32 devices in a mesh: groups: 2 (over y), patch: 4 (over z), view: 2 (over x), head: 2 (over core).
Axes of the slice: x: 2, y: 2, z: 4, core: 2. Of those that a mesh axis runs over, the one named last changes fastest.
Arguments:
- tokens: bfloat16 [8192, 768], P(('groups', 'patch', 'view', 'head')), parts along dimension 0, may hold values from -6 to 6
- w_kv: bfloat16 [768, 1536], replicated, may hold values from -0.21875 to 0.21875
- w_rate: bfloat16 [3, 768], replicated, may hold values from -0.21875 to 0.21875
- fast_weights: bfloat16 [512, 3, 3, 256], replicated, as said below
- queries: bfloat16 [8192, 768], P(('groups', 'patch', 'view', 'head')), parts along dimension 0, may hold values from -6 to 6
- w_query: bfloat16 [768, 768], replicated, may hold values from -0.21875 to 0.21875
- out_gain: bfloat16 [768], replicated, may hold values from 0.25 to 1.75
- w_out: bfloat16 [768, 768], replicated, may hold values from -0.21875 to 0.21875
Outputs:
- decoded: bfloat16 [8192, 768], P(('groups', 'patch', 'view', 'head')), parts along dimension 0
The draws below stay inside these ranges and needn't reach their ends.
There are 2 independent parts, one for each index of `groups`. The reference program is written for one: setup_inputs(seed, part) draws one part's arguments, and reference() takes and returns one part's arrays. A program takes and returns all parts, laid end to end along the dimension named above; an argument that names none is the same for every part. Nothing has to cross between parts.
Inputs may be any that keep to these rules, and one draw needn't show every extreme that they name: `fast_weights`: Real-valued entries.
All inputs are finite; a program needn't handle non-finite values.
Results may differ from the reference program's by a relative error of at most 0.035.
Values may be sent and summed in bfloat16 or wider, within the bound.
A program may use at most 64 MiB of HBM per device.

```python
import math
import jax
import jax.numpy as jnp
from jax import lax

HEADS = 3
HD = 256
FF = 512
D = 768
TOK_DEV = 256
QRY_DEV = 256
STEPS = 3
TOKENS = 4096
QUERIES = 4096
N_HEAD = 2


def draw_fast_weights(key, part):
    shape = (FF, 3, HEADS, HD)
    base = jnp.clip(jax.random.normal(key, shape, jnp.float32), -4.0, 4.0)
    rise = math.log(3.0)
    position = jnp.arange(FF, dtype=jnp.float32) / (FF - 1)
    factor = jnp.exp(rise * position)[:, None, None, None]
    return (base * factor * HD ** (-0.5)).astype(jnp.bfloat16)


def shard_levels(own_key, extent, shards, least, high):
    loudness = 1.0
    for dim, blocks in shards:
        heights = jax.random.uniform(jax.random.fold_in(jax.random.fold_in(own_key, 6), dim), (blocks,), jnp.float32, least / len(shards), high / len(shards))
        loudness = loudness * jnp.repeat(jnp.exp(heights), extent[dim] // blocks).reshape((-1,) + (1,) * (len(extent) - 1 - dim))
    return loudness


def normal_values(stream_key, dims, scale, most, shards=(), kind=jnp.bfloat16):
    entries = scale * jax.random.normal(stream_key, dims, jnp.float32)
    if shards:
        entries = entries * shard_levels(stream_key, dims, shards, -0.22, 0.18)
    return jnp.clip(entries, -most, most).astype(kind)


def setup_inputs(seed: int = 0, part: int = 0) -> dict:
    key_of = jax.random.split(jax.random.key(seed), 9)
    part_splits = jax.random.split(jax.random.fold_in(key_of[8], part), 9)
    return {
        "tokens": normal_values(part_splits[0], (TOKENS, D), 1.0, 6.0, ((0, 16),)),
        "w_kv": normal_values(key_of[1], (D, 2 * D), D ** -0.5, 0.21875),
        "w_rate": normal_values(key_of[2], (HEADS, D), D ** -0.5, 0.21875),
        "fast_weights": draw_fast_weights(jax.random.fold_in(key_of[8], 71), part),
        "queries": normal_values(part_splits[4], (QUERIES, D), 1.0, 6.0, ((0, 16),)),
        "w_query": normal_values(key_of[5], (D, D), D ** -0.5, 0.21875),
        "out_gain": jnp.clip(1.0 + 0.15 * jax.random.normal(key_of[6], (D,), jnp.float32), 0.25, 1.75).astype(jnp.bfloat16),
        "w_out": normal_values(key_of[7], (D, D), D ** -0.5, 0.21875),
    }


coef_a = 3.4445
coef_b = -4.775
coef_c = 2.0315
eta_rate = 3.0
eps_small = 1e-06

def unit_heads(raw):
    shaped = raw.reshape(raw.shape[0], HEADS, HD)
    return shaped / jnp.sqrt(lax.optimization_barrier(jnp.sum(shaped * shaped, -1, keepdims=True)) + eps_small)

def reference(tokens, w_kv, w_rate, fast_weights, queries, w_query, out_gain, w_out):
    fp = jnp.float32
    width = HEADS * HD
    fast = fast_weights.astype(fp)
    block = TOK_DEV * N_HEAD

    def grad_block(total, index):
        xrows = lax.dynamic_slice_in_dim(tokens, (index * block).astype(jnp.int32), block, 0)
        both = jnp.dot(xrows, w_kv, preferred_element_type=fp)
        keys = unit_heads(both[:, :width]).astype(jnp.bfloat16).astype(fp)
        rate = jax.nn.softplus(jnp.dot(xrows, w_rate.T, preferred_element_type=fp))
        scaled = (rate[:, :, None] * both[:, width:].reshape(-1, HEADS, HD)).astype(jnp.bfloat16).astype(fp)
        gate_pre = jnp.einsum('thd,nhd->hnt', keys, fast[:, 0])
        up_pre = jnp.einsum('thd,nhd->hnt', keys, fast[:, 1])
        sig = jax.nn.sigmoid(gate_pre)
        act = gate_pre * sig
        hidden = (act * up_pre).astype(jnp.bfloat16).astype(fp)
        back = jnp.einsum('thd,nhd->hnt', scaled, fast[:, 2])
        d_gate = (back * up_pre * sig * (1.0 + gate_pre * (1.0 - sig))).astype(jnp.bfloat16).astype(fp)
        d_up = (back * act).astype(jnp.bfloat16).astype(fp)
        g_gate = jnp.einsum('hnt,thd->nhd', d_gate, keys)
        g_up = jnp.einsum('hnt,thd->nhd', d_up, keys)
        g_down = jnp.einsum('hnt,thd->nhd', hidden, scaled)
        return (total + jnp.stack([g_gate, g_up, g_down], 1), None)
    grads, _ = lax.scan(grad_block, jnp.zeros((FF, 3, HEADS, HD), fp), jnp.arange(TOKENS // block, dtype=jnp.int32))
    total = lax.optimization_barrier(jnp.sum(grads * grads, axis=(0, 3)))
    ortho = (grads / (jnp.sqrt(total) + eps_small)[None, :, :, None]).astype(jnp.bfloat16)
    for step in range(STEPS):
        xf = ortho.astype(fp)
        gram = jnp.einsum('nkhi,nkhj->khij', xf, xf).astype(jnp.bfloat16).astype(fp)
        square = jnp.einsum('khij,khjl->khil', gram, gram)
        poly = (coef_b * gram + coef_c * square).astype(jnp.bfloat16).astype(fp)
        ortho = (coef_a * xf + jnp.einsum('nkhi,khij->nkhj', xf, poly)).astype(jnp.bfloat16)
    moved = fast + eta_rate * ortho.astype(fp)
    old_norm = jnp.sqrt(lax.optimization_barrier(jnp.sum(fast * fast, -1, keepdims=True)))
    new_norm = jnp.sqrt(lax.optimization_barrier(jnp.sum(moved * moved, -1, keepdims=True))) + eps_small
    fresh = (moved * old_norm / new_norm).astype(jnp.bfloat16).astype(fp)
    qblock = QRY_DEV * N_HEAD

    def decode_block(index):
        qrows = lax.dynamic_slice_in_dim(queries, (index * qblock).astype(jnp.int32), qblock, 0)
        qry = unit_heads(jnp.dot(qrows, w_query, preferred_element_type=fp)).astype(jnp.bfloat16).astype(fp)
        gate_pre = jnp.einsum('thd,nhd->hnt', qry, fresh[:, 0])
        up_pre = jnp.einsum('thd,nhd->hnt', qry, fresh[:, 1])
        q_hidden = (jax.nn.silu(gate_pre) * up_pre).astype(jnp.bfloat16).astype(fp)
        read = jnp.einsum('hnt,nhd->thd', q_hidden, fresh[:, 2])
        normed = read / jnp.sqrt(lax.optimization_barrier(jnp.mean(read * read, -1, keepdims=True)) + eps_small)
        normed = normed * out_gain.astype(fp).reshape(HEADS, HD)
        normed = normed.reshape(qblock, width).astype(jnp.bfloat16)
        return jnp.dot(normed, w_out, preferred_element_type=fp).astype(jnp.bfloat16)
    blocks = lax.map(decode_block, jnp.arange(QUERIES // qblock, dtype=jnp.int32))
    return blocks.reshape(QUERIES, width)
```

```python
import functools

import jax
import jax.numpy as jnp
from jax import lax
from jax.experimental import pallas as pl
from jax.experimental.pallas import tpu as pltpu
from jax.sharding import PartitionSpec as P

HEADS = 3
HD = 256
FF = 512
STEPS = 3
KINDS = 3
ROWS = KINDS * FF
D = HEADS * HD
MESH = pl.DeviceIdType.MESH

coef_a = 3.4445
coef_b = -4.775
coef_c = 2.0315
eta_rate = 3.0
eps_small = 1e-06
fp = jnp.float32
half_type = jnp.bfloat16


def dot_nn(a, b):
    return lax.dot_general(a, b, (((1,), (0,)), ((), ())), preferred_element_type=fp)


def dot_nt(a, b):
    return lax.dot_general(a, b, (((1,), (1,)), ((), ())), preferred_element_type=fp)


def dot_tn(a, b):
    return lax.dot_general(a, b, (((0,), (0,)), ((), ())), preferred_element_type=fp)


def unit(raw):
    return (raw * lax.rsqrt(jnp.sum(raw * raw, -1, keepdims=True) + eps_small)).astype(half_type)


def head_columns(kind, head):
    start = (kind * HEADS + head) * HD
    return slice(start, start + HD)


def kernel(
    n_view, n_patch, rows,
    tokens, w_kv, w_rate, fast, queries, w_query, gain, w_out, out,
    keys, scaled, qry, grad, core_in, mid, view_in, low, patch_in, full, acc, send, recv,
):
    core, view, patch = lax.axis_index("head"), lax.axis_index("view"), lax.axis_index("patch")
    half = rows // 2
    part = half // n_view
    piece = part // n_patch

    views = [(d, d, lax.rem(view + d, n_view)) for d in range(1, n_view)]
    patches = [(d, n_view - 1 + d, lax.rem(patch + d, n_patch)) for d in range(1, n_patch)]

    barrier = pltpu.get_barrier_semaphore()
    pl.semaphore_signal(barrier, inc=1, device_id={"head": 1 - core}, device_id_type=MESH)
    for _, _, to in views:
        pl.semaphore_signal(barrier, inc=1, device_id={"view": to}, device_id_type=MESH)
    for _, _, to in patches:
        pl.semaphore_signal(barrier, inc=1, device_id={"patch": to}, device_id_type=MESH)

    started = []

    def span(start, size):
        return pl.ds(pl.multiple_of(start, 16), size)

    def launch(head, way, slot, source, target, where):
        copy = pltpu.make_async_remote_copy(
            src_ref=source, dst_ref=target,
            send_sem=send.at[head, way, slot], recv_sem=recv.at[head, way, slot],
            device_id=where, device_id_type=MESH,
        )
        copy.start()
        started.append(copy)
        return copy

    def arrive(copies):
        for copy in copies:
            copy.wait_recv()

    hops = {}

    def gradient(h):
        fast_gate = fast[:, head_columns(0, h)]
        fast_up = fast[:, head_columns(1, h)]
        fast_down = fast[:, head_columns(2, h)]
        key, val = keys[h], scaled[h]
        gate_pre = dot_nt(fast_gate, key)
        up_pre = dot_nt(fast_up, key)
        back = dot_nt(fast_down, val)
        sig = jax.nn.sigmoid(gate_pre)
        act = gate_pre * sig
        hidden = (act * up_pre).astype(half_type)
        d_gate = (back * up_pre * sig * (1.0 + gate_pre * (1.0 - sig))).astype(half_type)
        d_up = (back * act).astype(half_type)
        grad[h, 0:FF] = dot_nn(d_gate, key).astype(half_type)
        grad[h, FF:2 * FF] = dot_nn(d_up, key).astype(half_type)
        grad[h, 2 * FF:3 * FF] = dot_nn(hidden, val).astype(half_type)
        if rows > ROWS:
            grad[h, ROWS:rows] = jnp.zeros((rows - ROWS, HD), half_type)

    def scatter_core(h):
        hops[h, 0] = [
            launch(h, 0, 0, grad.at[h, span((1 - core) * half, half)], core_in.at[h], {"head": 1 - core})
        ]

    def scatter_view(h):
        arrive(hops[h, 0])
        mid[h] = (grad[h, span(core * half, half)].astype(fp) + core_in[h].astype(fp)).astype(half_type)
        hops[h, 1] = [
            launch(h, 0, slot, mid.at[h, span(to * part, part)], view_in.at[h, d - 1], {"view": to})
            for d, slot, to in views
        ]

    def scatter_patch(h):
        arrive(hops[h, 1])
        total = mid[h, span(view * part, part)].astype(fp)
        for d in range(n_view - 1):
            total = total + view_in[h, d].astype(fp)
        low[h] = total.astype(half_type)
        hops[h, 2] = [
            launch(h, 0, slot, low.at[h, span(to * piece, piece)], patch_in.at[h, d - 1], {"patch": to})
            for d, slot, to in patches
        ]

    def gather_patch(h):
        arrive(hops[h, 2])
        total = low[h, span(patch * piece, piece)].astype(fp)
        for d in range(n_patch - 1):
            total = total + patch_in[h, d].astype(fp)
        own = span(core * half + view * part + patch * piece, piece)
        full[h, own] = total.astype(half_type)
        hops[h, 3] = [
            launch(h, 1, slot, full.at[h, own], full.at[h, own], {"patch": to})
            for _, slot, to in patches
        ]

    def gather_view(h):
        arrive(hops[h, 3])
        own = span(core * half + view * part, part)
        hops[h, 4] = [
            launch(h, 1, slot, full.at[h, own], full.at[h, own], {"view": to})
            for _, slot, to in views
        ]

    def gather_core(h):
        arrive(hops[h, 4])
        own = span(core * half, half)
        hops[h, 5] = [launch(h, 1, 0, full.at[h, own], full.at[h, own], {"head": 1 - core})]

    def start_point(h):
        arrive(hops[h, 5])
        begin = []
        for kind in range(KINDS):
            summed = full[h, kind * FF:(kind + 1) * FF].astype(fp)
            norm = jnp.sqrt(jnp.sum(summed * summed, keepdims=True)) + eps_small
            begin.append((summed * (1.0 / norm)).astype(half_type))
        return begin

    def newton(ortho):
        grams = [dot_tn(x, x).astype(half_type) for x in ortho]
        polys = [
            (coef_b * g.astype(fp) + coef_c * dot_nn(g, g)).astype(half_type) for g in grams
        ]
        return [
            (coef_a * x.astype(fp) + dot_nn(x, p)).astype(half_type) for x, p in zip(ortho, polys)
        ]

    def renorm(h, ortho):
        fresh = []
        for kind in range(KINDS):
            old = fast[:, head_columns(kind, h)].astype(fp)
            moved = old + eta_rate * ortho[kind].astype(fp)
            old_norm = jnp.sqrt(jnp.sum(old * old, -1, keepdims=True))
            new_norm = jnp.sqrt(jnp.sum(moved * moved, -1, keepdims=True)) + eps_small
            fresh.append((moved * (old_norm / new_norm)).astype(half_type))
        return fresh

    def decode(h, fresh):
        gate_pre = dot_nt(qry[h], fresh[0])
        up_pre = dot_nt(qry[h], fresh[1])
        q_hidden = (gate_pre * jax.nn.sigmoid(gate_pre) * up_pre).astype(half_type)
        read = dot_nn(q_hidden, fresh[2])
        normed = read * lax.rsqrt(jnp.mean(read * read, -1, keepdims=True) + eps_small)
        normed = (normed * gain[:, h * HD:(h + 1) * HD].astype(fp)).astype(half_type)
        term = dot_nn(normed, w_out[h * HD:(h + 1) * HD, :])
        if h == 0:
            acc[...] = term
        elif h < HEADS - 1:
            acc[...] += term
        else:
            out[...] = (acc[...] + term).astype(half_type)

    rate_pre = dot_nt(tokens[...], w_rate[...])
    rate = jnp.maximum(rate_pre, 0.0) + jnp.log1p(jnp.exp(-jnp.abs(rate_pre)))
    for h in range(HEADS):
        keys[h] = unit(dot_nn(tokens[...], w_kv[:, h * HD:(h + 1) * HD]))
        values = dot_nn(tokens[...], w_kv[:, D + h * HD:D + (h + 1) * HD])
        scaled[h] = (rate[:, h:h + 1] * values).astype(half_type)

    gradient(0)
    pl.semaphore_wait(barrier, 1 + len(views) + len(patches))
    scatter_core(0)
    gradient(1)
    scatter_core(1)
    scatter_view(0)
    gradient(2)
    scatter_core(2)
    scatter_view(1)
    for h in range(HEADS):
        qry[h] = unit(dot_nn(queries[...], w_query[:, h * HD:(h + 1) * HD]))
    scatter_view(2)
    scatter_patch(0)
    scatter_patch(1)
    gather_patch(0)
    scatter_patch(2)
    gather_patch(1)
    gather_view(0)
    gather_patch(2)
    gather_view(1)
    gather_core(0)
    ortho = newton(start_point(0))
    gather_core(1)
    ortho = newton(newton(ortho))
    gather_view(2)
    decode(0, renorm(0, ortho))
    ortho = newton(start_point(1))
    gather_core(2)
    decode(1, renorm(1, newton(newton(ortho))))
    decode(2, renorm(2, newton(newton(newton(start_point(2))))))
    for copy in started:
        copy.wait_send()


def solution(mesh):
    n_view, n_patch = mesh.shape["view"], mesh.shape["patch"]
    unit_rows = 16 * 2 * n_view * n_patch
    rows = -(-ROWS // unit_rows) * unit_rows
    half = rows // 2
    part = half // n_view
    piece = part // n_patch
    hop_count = n_view + n_patch - 1

    def local(tokens, w_kv, w_rate, fast_weights, queries, w_query, out_gain, w_out):
        count, width = tokens.shape
        asked = queries.shape[0]
        return pl.pallas_call(
            functools.partial(kernel, n_view, n_patch, rows),
            out_shape=jax.ShapeDtypeStruct((asked, width), half_type),
            in_specs=[pl.BlockSpec(memory_space=pltpu.VMEM)] * 8,
            out_specs=pl.BlockSpec(memory_space=pltpu.VMEM),
            scratch_shapes=[
                pltpu.VMEM((HEADS, count, HD), half_type),
                pltpu.VMEM((HEADS, count, HD), half_type),
                pltpu.VMEM((HEADS, asked, HD), half_type),
                pltpu.VMEM((HEADS, rows, HD), half_type),
                pltpu.VMEM((HEADS, half, HD), half_type),
                pltpu.VMEM((HEADS, half, HD), half_type),
                pltpu.VMEM((HEADS, n_view - 1, part, HD), half_type),
                pltpu.VMEM((HEADS, part, HD), half_type),
                pltpu.VMEM((HEADS, n_patch - 1, piece, HD), half_type),
                pltpu.VMEM((HEADS, rows, HD), half_type),
                pltpu.VMEM((asked, width), fp),
                pltpu.SemaphoreType.DMA((HEADS, 2, hop_count)),
                pltpu.SemaphoreType.DMA((HEADS, 2, hop_count)),
            ],
            compiler_params=pltpu.CompilerParams(
                collective_id=0, has_side_effects=True, vmem_limit_bytes=48 * 1024 * 1024
            ),
        )(
            tokens, w_kv, w_rate, fast_weights.reshape(FF, KINDS * HEADS * HD),
            queries, w_query, out_gain.reshape(1, width), w_out,
        )

    shard = P(("groups", "patch", "view", "head"), None)
    in_specs = (shard, P(), P(), P(), shard, P(), P(), P())
    return jax.shard_map(local, mesh=mesh, in_specs=in_specs, out_specs=shard, check_vma=False)
```

```python
import functools

import jax
import jax.numpy as jnp
from jax import lax
from jax.experimental import pallas as pl
from jax.experimental.pallas import tpu as pltpu
from jax.sharding import PartitionSpec as P

HEADS = 3
HD = 256
FF = 512
STEPS = 3
KINDS = 3
MATS = KINDS * HEADS
D = HEADS * HD
MESH = pl.DeviceIdType.MESH

coef_a = 3.4445
coef_b = -4.775
coef_c = 2.0315
eta_rate = 3.0
eps_small = 1e-06
fp = jnp.float32
half_type = jnp.bfloat16


def dot_nn(a, b):
    return lax.dot_general(a, b, (((1,), (0,)), ((), ())), preferred_element_type=fp)


def dot_nt(a, b):
    return lax.dot_general(a, b, (((1,), (1,)), ((), ())), preferred_element_type=fp)


def dot_tn(a, b):
    return lax.dot_general(a, b, (((0,), (0,)), ((), ())), preferred_element_type=fp)


def unit(raw):
    return (raw * lax.rsqrt(jnp.sum(raw * raw, -1, keepdims=True) + eps_small)).astype(half_type)


def kernel(
    n_view, n_patch,
    tokens_hbm, w_kv_hbm, w_rate, fast_hbm, queries_hbm, w_query_hbm, gain, w_out_hbm, out,
    tokens, w_kv, fast, queries, w_query, w_out,
    keys, scaled, qry, grad, core_in, mid, view_in, low, patch_in, full, fresh, acc,
    load, send, recv,
):
    core, view, patch = lax.axis_index("head"), lax.axis_index("view"), lax.axis_index("patch")
    piece = FF // n_patch
    patches = [(d, lax.rem(patch + d, n_patch)) for d in range(1, n_patch)]
    loads = []

    def fetch(source, target):
        copy = pltpu.make_async_copy(source, target, load.at[len(loads)])
        copy.start()
        loads.append(copy)
        return copy

    get_tokens = fetch(tokens_hbm, tokens)
    get_kv = fetch(w_kv_hbm, w_kv)
    get_fast = [fetch(fast_hbm.at[:, h], fast.at[:, h]) for h in range(HEADS)]
    get_query = [fetch(queries_hbm, queries), fetch(w_query_hbm, w_query)]
    get_out = fetch(w_out_hbm, w_out)

    barrier = pltpu.get_barrier_semaphore()
    pl.semaphore_signal(barrier, inc=1, device_id={"head": 1 - core}, device_id_type=MESH)
    for d in range(1, n_view):
        pl.semaphore_signal(
            barrier, inc=1, device_id={"view": lax.rem(view + d, n_view)}, device_id_type=MESH
        )
    for _, to in patches:
        pl.semaphore_signal(barrier, inc=1, device_id={"patch": to}, device_id_type=MESH)

    core_sum, core_share = 0, 1
    view_sum = 2
    view_share = view_sum + n_view - 1
    patch_sum = view_share + n_view - 1
    patch_share = patch_sum + n_patch - 1

    def owner(m):
        slot = m % (2 * n_view)
        return slot % n_view, slot // n_view

    def remote(m, slot, source, target, where):
        return pltpu.make_async_remote_copy(
            src_ref=source, dst_ref=target, send_sem=send.at[m, slot], recv_sem=recv.at[m, slot],
            device_id=where, device_id_type=MESH,
        )

    def sum_over_core(m):
        return remote(m, core_sum, grad.at[m], core_in.at[m], {"head": 1 - core})

    def sum_over_view(m, d):
        return remote(m, view_sum + d - 1, mid.at[m], view_in.at[m, d - 1], {"view": owner(m)[0]})

    def sum_over_patch(m, d, to):
        start = pl.multiple_of(to * piece, 16)
        return remote(
            m, patch_sum + d - 1, low.at[m, pl.ds(start, piece)], patch_in.at[m, d - 1], {"patch": to}
        )

    def share_over_patch(m, d, to):
        own = full.at[m, pl.ds(pl.multiple_of(patch * piece, 16), piece)]
        return remote(m, patch_share + d - 1, own, own, {"patch": to})

    def share_over_view(m, d):
        to = (owner(m)[0] + d) % n_view
        return remote(m, view_share + d - 1, fresh.at[m], fresh.at[m], {"view": to})

    def share_over_core(m):
        return remote(m, core_share, fresh.at[m], fresh.at[m], {"head": 1 - core})

    def at_owner(m):
        return jnp.logical_and(core == owner(m)[1], view == owner(m)[0])

    def at_view(m, v):
        return jnp.logical_and(core == owner(m)[1], view == v % n_view)

    def gradient(h):
        get_fast[h].wait()
        key, val = keys[h], scaled[h]
        gate_pre = dot_nt(fast[0, h], key)
        up_pre = dot_nt(fast[1, h], key)
        back = dot_nt(fast[2, h], val)
        sig = jax.nn.sigmoid(gate_pre)
        act = gate_pre * sig
        hidden = (act * up_pre).astype(half_type)
        d_gate = (back * up_pre * sig * (1.0 + gate_pre * (1.0 - sig))).astype(half_type)
        d_up = (back * act).astype(half_type)
        grad[h * KINDS] = dot_nn(d_gate, key).astype(half_type)
        grad[h * KINDS + 1] = dot_nn(d_up, key).astype(half_type)
        grad[h * KINDS + 2] = dot_nn(hidden, val).astype(half_type)

    def stage_core(m):
        @pl.when(core != owner(m)[1])
        def _():
            sum_over_core(m).start()

    def stage_view(m):
        @pl.when(core == owner(m)[1])
        def _():
            sum_over_core(m).wait_recv()
            mid[m] = (grad[m].astype(fp) + core_in[m].astype(fp)).astype(half_type)

        for d in range(1, n_view):
            @pl.when(at_view(m, owner(m)[0] - d))
            def _():
                sum_over_view(m, d).start()

    def stage_patch(m):
        @pl.when(at_owner(m))
        def _():
            total = mid[m].astype(fp)
            for d in range(1, n_view):
                sum_over_view(m, d).wait_recv()
                total = total + view_in[m, d - 1].astype(fp)
            low[m] = total.astype(half_type)
            for d, to in patches:
                sum_over_patch(m, d, to).start()

    def stage_gather(m):
        @pl.when(at_owner(m))
        def _():
            own = pl.ds(pl.multiple_of(patch * piece, 16), piece)
            total = low[m, own].astype(fp)
            for d, to in patches:
                sum_over_patch(m, d, to).wait_recv()
                total = total + patch_in[m, d - 1].astype(fp)
            full[m, own] = total.astype(half_type)
            for d, to in patches:
                share_over_patch(m, d, to).start()

    def newton(x):
        gram = dot_tn(x, x).astype(half_type)
        poly = (coef_b * gram.astype(fp) + coef_c * dot_nn(gram, gram)).astype(half_type)
        return (coef_a * x.astype(fp) + dot_nn(x, poly)).astype(half_type)

    def stage_update(m):
        @pl.when(at_owner(m))
        def _():
            for d, to in patches:
                share_over_patch(m, d, to).wait_recv()
            summed = full[m].astype(fp)
            norm = jnp.sqrt(jnp.sum(summed * summed, keepdims=True)) + eps_small
            ortho = (summed * (1.0 / norm)).astype(half_type)
            for _ in range(STEPS):
                ortho = newton(ortho)
            old = fast[m % KINDS, m // KINDS].astype(fp)
            moved = old + eta_rate * ortho.astype(fp)
            old_norm = jnp.sqrt(jnp.sum(old * old, -1, keepdims=True))
            new_norm = jnp.sqrt(jnp.sum(moved * moved, -1, keepdims=True)) + eps_small
            fresh[m] = (moved * (old_norm / new_norm)).astype(half_type)
            for d in range(1, n_view):
                share_over_view(m, d).start()
            share_over_core(m).start()

    def stage_spread(m):
        for d in range(1, n_view):
            @pl.when(at_view(m, owner(m)[0] + d))
            def _():
                share_over_view(m, d).wait_recv()
                share_over_core(m).start()

    def decode(h):
        for m in range(h * KINDS, (h + 1) * KINDS):
            @pl.when(core != owner(m)[1])
            def _():
                share_over_core(m).wait_recv()
        gate_pre = dot_nt(qry[h], fresh[h * KINDS])
        up_pre = dot_nt(qry[h], fresh[h * KINDS + 1])
        q_hidden = (gate_pre * jax.nn.sigmoid(gate_pre) * up_pre).astype(half_type)
        read = dot_nn(q_hidden, fresh[h * KINDS + 2])
        normed = read * lax.rsqrt(jnp.mean(read * read, -1, keepdims=True) + eps_small)
        normed = (normed * gain[:, h * HD:(h + 1) * HD].astype(fp)).astype(half_type)
        term = dot_nn(normed, w_out[h * HD:(h + 1) * HD, :])
        if h == 0:
            acc[...] = term
        elif h < HEADS - 1:
            acc[...] += term
        else:
            out[...] = (acc[...] + term).astype(half_type)

    def finish(m):
        @pl.when(core != owner(m)[1])
        def _():
            sum_over_core(m).wait_send()

        for d in range(1, n_view):
            @pl.when(at_view(m, owner(m)[0] - d))
            def _():
                sum_over_view(m, d).wait_send()

        @pl.when(at_owner(m))
        def _():
            for d, to in patches:
                sum_over_patch(m, d, to).wait_send()
                share_over_patch(m, d, to).wait_send()
            for d in range(1, n_view):
                share_over_view(m, d).wait_send()

        @pl.when(core == owner(m)[1])
        def _():
            share_over_core(m).wait_send()

    get_tokens.wait()
    rate_pre = dot_nt(tokens[...], w_rate[...])
    rate = jnp.maximum(rate_pre, 0.0) + jnp.log1p(jnp.exp(-jnp.abs(rate_pre)))
    get_kv.wait()
    first, second, last = [range(h * KINDS, (h + 1) * KINDS) for h in range(HEADS)]

    def project(h):
        keys[h] = unit(dot_nn(tokens[...], w_kv[:, h * HD:(h + 1) * HD]))
        values = dot_nn(tokens[...], w_kv[:, D + h * HD:D + (h + 1) * HD])
        scaled[h] = (rate[:, h:h + 1] * values).astype(half_type)

    def run(stage, chosen):
        for m in chosen:
            stage(m)

    project(0)
    gradient(0)
    pl.semaphore_wait(barrier, n_view + n_patch - 1)
    run(stage_core, first)
    project(1)
    run(stage_view, first)
    gradient(1)
    run(stage_core, second)
    project(2)
    run(stage_view, second)
    gradient(2)
    run(stage_core, last)
    for copy in get_query:
        copy.wait()
    for h in range(HEADS):
        qry[h] = unit(dot_nn(queries[...], w_query[:, h * HD:(h + 1) * HD]))
        if h == 0:
            run(stage_view, last)
    get_out.wait()
    early, late, rest = range(0, 4), range(4, 8), range(8, MATS)
    run(stage_patch, early)
    run(stage_gather, early)
    run(stage_patch, late)
    run(stage_update, early)
    run(stage_gather, late)
    run(stage_patch, rest)
    run(stage_spread, early)
    run(stage_update, late)
    run(stage_gather, rest)
    decode(0)
    run(stage_spread, late)
    run(stage_update, rest)
    decode(1)
    run(stage_spread, rest)
    decode(2)
    run(finish, range(MATS))


def solution(mesh):
    n_view, n_patch = mesh.shape["view"], mesh.shape["patch"]
    piece = FF // n_patch
    slots = 2 * (n_view + n_patch - 1)

    def local(tokens, w_kv, w_rate, fast_weights, queries, w_query, out_gain, w_out):
        count, width = tokens.shape
        asked = queries.shape[0]
        vmem = pl.BlockSpec(memory_space=pltpu.VMEM)
        hbm = pl.BlockSpec(memory_space=pl.ANY)
        whole = pltpu.VMEM((MATS, FF, HD), half_type)
        return pl.pallas_call(
            functools.partial(kernel, n_view, n_patch),
            out_shape=jax.ShapeDtypeStruct((asked, width), half_type),
            in_specs=[hbm, hbm, vmem, hbm, hbm, hbm, vmem, hbm],
            out_specs=vmem,
            scratch_shapes=[
                pltpu.VMEM((count, width), half_type),
                pltpu.VMEM((width, 2 * width), half_type),
                pltpu.VMEM((KINDS, HEADS, FF, HD), half_type),
                pltpu.VMEM((asked, width), half_type),
                pltpu.VMEM((width, width), half_type),
                pltpu.VMEM((width, width), half_type),
                pltpu.VMEM((HEADS, count, HD), half_type),
                pltpu.VMEM((HEADS, count, HD), half_type),
                pltpu.VMEM((HEADS, asked, HD), half_type),
                whole,
                whole,
                whole,
                pltpu.VMEM((MATS, n_view - 1, FF, HD), half_type),
                whole,
                pltpu.VMEM((MATS, n_patch - 1, piece, HD), half_type),
                whole,
                whole,
                pltpu.VMEM((asked, width), fp),
                pltpu.SemaphoreType.DMA((5 + HEADS,)),
                pltpu.SemaphoreType.DMA((MATS, slots)),
                pltpu.SemaphoreType.DMA((MATS, slots)),
            ],
            compiler_params=pltpu.CompilerParams(
                collective_id=0, has_side_effects=True, vmem_limit_bytes=56 * 1024 * 1024
            ),
        )(
            tokens, w_kv, w_rate, jnp.transpose(fast_weights, (1, 2, 0, 3)),
            queries, w_query, out_gain.reshape(1, width), w_out,
        )

    shard = P(("groups", "patch", "view", "head"), None)
    in_specs = (shard, P(), P(), P(), shard, P(), P(), P())
    return jax.shard_map(local, mesh=mesh, in_specs=in_specs, out_specs=shard, check_vma=False)
```

```python
import functools

import jax
import jax.numpy as jnp
from jax import lax
from jax.experimental import pallas as pl
from jax.experimental.pallas import tpu as pltpu
from jax.sharding import PartitionSpec as P

HEADS = 3
HD = 256
FF = 512
STEPS = 3
KINDS = 3
MATS = KINDS * HEADS
D = HEADS * HD
MESH = pl.DeviceIdType.MESH

coef_a = 3.4445
coef_b = -4.775
coef_c = 2.0315
eta_rate = 3.0
eps_small = 1e-06
fp = jnp.float32
half_type = jnp.bfloat16


def dot_nn(a, b):
    return lax.dot_general(a, b, (((1,), (0,)), ((), ())), preferred_element_type=fp)


def dot_nt(a, b):
    return lax.dot_general(a, b, (((1,), (1,)), ((), ())), preferred_element_type=fp)


def dot_tn(a, b):
    return lax.dot_general(a, b, (((0,), (0,)), ((), ())), preferred_element_type=fp)


def unit(raw):
    return (raw * lax.rsqrt(jnp.sum(raw * raw, -1, keepdims=True) + eps_small)).astype(half_type)


def kernel(
    n_view, n_patch,
    tokens_hbm, w_kv_hbm, w_rate, fast_hbm, queries_hbm, w_query_hbm, gain, w_out_hbm, out,
    tokens, w_kv, fast, queries, w_query, w_out,
    keys, scaled, qry, grad, core_in, mid, view_in, low, patch_in, full, fresh, acc,
    load, send, recv,
):
    core, view, patch = lax.axis_index("head"), lax.axis_index("view"), lax.axis_index("patch")
    piece = FF // n_patch
    patches = [(d, lax.rem(patch + d, n_patch)) for d in range(1, n_patch)]
    loads = []

    def fetch(source, target):
        copy = pltpu.make_async_copy(source, target, load.at[len(loads)])
        copy.start()
        loads.append(copy)
        return copy

    get_tokens = fetch(tokens_hbm, tokens)
    get_kv, get_fast = [], []
    for h in range(HEADS):
        get_kv.append([
            fetch(w_kv_hbm.at[:, start:start + HD], w_kv.at[:, start:start + HD])
            for start in (h * HD, D + h * HD)
        ])
        get_fast.append(fetch(fast_hbm.at[:, h], fast.at[:, h]))
    get_query = [fetch(queries_hbm, queries), fetch(w_query_hbm, w_query)]
    get_out = fetch(w_out_hbm, w_out)

    barrier = pltpu.get_barrier_semaphore()
    pl.semaphore_signal(barrier, inc=1, device_id={"head": 1 - core}, device_id_type=MESH)
    for d in range(1, n_view):
        pl.semaphore_signal(
            barrier, inc=1, device_id={"view": lax.rem(view + d, n_view)}, device_id_type=MESH
        )
    for _, to in patches:
        pl.semaphore_signal(barrier, inc=1, device_id={"patch": to}, device_id_type=MESH)

    core_sum, core_share = 0, 1
    view_sum = 2
    view_share = view_sum + n_view - 1
    patch_sum = view_share + n_view - 1
    patch_share = patch_sum + n_patch - 1

    def owner(m):
        slot = m % (2 * n_view)
        return slot % n_view, slot // n_view

    def remote(m, slot, source, target, where):
        return pltpu.make_async_remote_copy(
            src_ref=source, dst_ref=target, send_sem=send.at[m, slot], recv_sem=recv.at[m, slot],
            device_id=where, device_id_type=MESH,
        )

    def sum_over_core(m):
        return remote(m, core_sum, grad.at[m], core_in.at[m], {"head": 1 - core})

    def sum_over_view(m, d):
        return remote(m, view_sum + d - 1, mid.at[m], view_in.at[m, d - 1], {"view": owner(m)[0]})

    def sum_over_patch(m, d, to):
        start = pl.multiple_of(to * piece, 16)
        return remote(
            m, patch_sum + d - 1, low.at[m, pl.ds(start, piece)], patch_in.at[m, d - 1], {"patch": to}
        )

    def share_over_patch(m, d, to):
        own = full.at[m, pl.ds(pl.multiple_of(patch * piece, 16), piece)]
        return remote(m, patch_share + d - 1, own, own, {"patch": to})

    def share_over_view(m, d):
        to = (owner(m)[0] + d) % n_view
        return remote(m, view_share + d - 1, fresh.at[m], fresh.at[m], {"view": to})

    def share_over_core(m):
        return remote(m, core_share, fresh.at[m], fresh.at[m], {"head": 1 - core})

    def at_owner(m):
        return jnp.logical_and(core == owner(m)[1], view == owner(m)[0])

    def at_view(m, v):
        return jnp.logical_and(core == owner(m)[1], view == v % n_view)

    def gradient(h):
        get_fast[h].wait()
        key, val = keys[h], scaled[h]
        gate_pre = dot_nt(fast[0, h], key)
        up_pre = dot_nt(fast[1, h], key)
        back = dot_nt(fast[2, h], val)
        sig = jax.nn.sigmoid(gate_pre)
        act = gate_pre * sig
        hidden = (act * up_pre).astype(half_type)
        d_gate = (back * up_pre * sig * (1.0 + gate_pre * (1.0 - sig))).astype(half_type)
        d_up = (back * act).astype(half_type)
        grad[h * KINDS] = dot_nn(d_gate, key).astype(half_type)
        grad[h * KINDS + 1] = dot_nn(d_up, key).astype(half_type)
        grad[h * KINDS + 2] = dot_nn(hidden, val).astype(half_type)

    def stage_core(m):
        @pl.when(core != owner(m)[1])
        def _():
            sum_over_core(m).start()

    def stage_view(m):
        @pl.when(core == owner(m)[1])
        def _():
            sum_over_core(m).wait_recv()
            mid[m] = (grad[m].astype(fp) + core_in[m].astype(fp)).astype(half_type)

        for d in range(1, n_view):
            @pl.when(at_view(m, owner(m)[0] - d))
            def _():
                sum_over_view(m, d).start()

    def stage_patch(m):
        @pl.when(at_owner(m))
        def _():
            total = mid[m].astype(fp)
            for d in range(1, n_view):
                sum_over_view(m, d).wait_recv()
                total = total + view_in[m, d - 1].astype(fp)
            low[m] = total.astype(half_type)
            for d, to in patches:
                sum_over_patch(m, d, to).start()

    def stage_gather(m):
        @pl.when(at_owner(m))
        def _():
            own = pl.ds(pl.multiple_of(patch * piece, 16), piece)
            total = low[m, own].astype(fp)
            for d, to in patches:
                sum_over_patch(m, d, to).wait_recv()
                total = total + patch_in[m, d - 1].astype(fp)
            full[m, own] = total.astype(half_type)
            for d, to in patches:
                share_over_patch(m, d, to).start()

    def newton(x):
        gram = dot_tn(x, x).astype(half_type)
        poly = (coef_b * gram.astype(fp) + coef_c * dot_nn(gram, gram)).astype(half_type)
        return (coef_a * x.astype(fp) + dot_nn(x, poly)).astype(half_type)

    def stage_update(m):
        @pl.when(at_owner(m))
        def _():
            for d, to in patches:
                share_over_patch(m, d, to).wait_recv()
            summed = full[m].astype(fp)
            norm = jnp.sqrt(jnp.sum(summed * summed, keepdims=True)) + eps_small
            ortho = (summed * (1.0 / norm)).astype(half_type)
            for _ in range(STEPS):
                ortho = newton(ortho)
            old = fast[m % KINDS, m // KINDS].astype(fp)
            moved = old + eta_rate * ortho.astype(fp)
            old_norm = jnp.sqrt(jnp.sum(old * old, -1, keepdims=True))
            new_norm = jnp.sqrt(jnp.sum(moved * moved, -1, keepdims=True)) + eps_small
            fresh[m] = (moved * (old_norm / new_norm)).astype(half_type)
            for d in range(1, n_view):
                share_over_view(m, d).start()
            share_over_core(m).start()

    def stage_spread(m):
        for d in range(1, n_view):
            @pl.when(at_view(m, owner(m)[0] + d))
            def _():
                share_over_view(m, d).wait_recv()
                share_over_core(m).start()

    def decode(h):
        for m in range(h * KINDS, (h + 1) * KINDS):
            @pl.when(core != owner(m)[1])
            def _():
                share_over_core(m).wait_recv()
        gate_pre = dot_nt(qry[h], fresh[h * KINDS])
        up_pre = dot_nt(qry[h], fresh[h * KINDS + 1])
        q_hidden = (gate_pre * jax.nn.sigmoid(gate_pre) * up_pre).astype(half_type)
        read = dot_nn(q_hidden, fresh[h * KINDS + 2])
        normed = read * lax.rsqrt(jnp.mean(read * read, -1, keepdims=True) + eps_small)
        normed = (normed * gain[h * HD:(h + 1) * HD].astype(fp)[None, :]).astype(half_type)
        term = dot_nn(normed, w_out[h * HD:(h + 1) * HD, :])
        if h == 0:
            acc[...] = term
        elif h < HEADS - 1:
            acc[...] += term
        else:
            out[...] = (acc[...] + term).astype(half_type)

    def finish(m):
        @pl.when(core != owner(m)[1])
        def _():
            sum_over_core(m).wait_send()

        for d in range(1, n_view):
            @pl.when(at_view(m, owner(m)[0] - d))
            def _():
                sum_over_view(m, d).wait_send()

        @pl.when(at_owner(m))
        def _():
            for d, to in patches:
                sum_over_patch(m, d, to).wait_send()
                share_over_patch(m, d, to).wait_send()
            for d in range(1, n_view):
                share_over_view(m, d).wait_send()

        @pl.when(core == owner(m)[1])
        def _():
            share_over_core(m).wait_send()

    get_tokens.wait()
    rate_pre = dot_nt(tokens[...], w_rate[...])
    rate = jnp.maximum(rate_pre, 0.0) + jnp.log1p(jnp.exp(-jnp.abs(rate_pre)))
    first, second, last = [range(h * KINDS, (h + 1) * KINDS) for h in range(HEADS)]

    def project(h):
        for copy in get_kv[h]:
            copy.wait()
        keys[h] = unit(dot_nn(tokens[...], w_kv[:, h * HD:(h + 1) * HD]))
        values = dot_nn(tokens[...], w_kv[:, D + h * HD:D + (h + 1) * HD])
        scaled[h] = (rate[:, h:h + 1] * values).astype(half_type)

    def run(stage, chosen):
        for m in chosen:
            stage(m)

    project(0)
    gradient(0)
    pl.semaphore_wait(barrier, n_view + n_patch - 1)
    run(stage_core, first)
    project(1)
    run(stage_view, first)
    gradient(1)
    run(stage_core, second)
    project(2)
    run(stage_view, second)
    gradient(2)
    run(stage_core, last)
    for copy in get_query:
        copy.wait()
    for h in range(HEADS):
        qry[h] = unit(dot_nn(queries[...], w_query[:, h * HD:(h + 1) * HD]))
        if h == 0:
            run(stage_view, last)
    get_out.wait()
    early, late, rest = range(0, 4), range(4, 8), range(8, MATS)
    run(stage_patch, early)
    run(stage_gather, early)
    run(stage_patch, late)
    run(stage_gather, late)
    run(stage_patch, rest)
    run(stage_update, early)
    run(stage_gather, rest)
    run(stage_update, late)
    run(stage_spread, early)
    run(stage_update, rest)
    run(stage_spread, late)
    decode(0)
    decode(1)
    run(stage_spread, rest)
    decode(2)
    run(finish, range(MATS))


def solution(mesh):
    n_view, n_patch = mesh.shape["view"], mesh.shape["patch"]
    piece = FF // n_patch
    slots = 2 * (n_view + n_patch - 1)

    def local(tokens, w_kv, w_rate, fast_weights, queries, w_query, out_gain, w_out):
        count, width = tokens.shape
        asked = queries.shape[0]
        vmem = pl.BlockSpec(memory_space=pltpu.VMEM)
        hbm = pl.BlockSpec(memory_space=pl.ANY)
        whole = pltpu.VMEM((MATS, FF, HD), half_type)
        return pl.pallas_call(
            functools.partial(kernel, n_view, n_patch),
            out_shape=jax.ShapeDtypeStruct((asked, width), half_type),
            in_specs=[hbm, hbm, vmem, hbm, hbm, hbm, vmem, hbm],
            out_specs=vmem,
            scratch_shapes=[
                pltpu.VMEM((count, width), half_type),
                pltpu.VMEM((width, 2 * width), half_type),
                pltpu.VMEM((KINDS, HEADS, FF, HD), half_type),
                pltpu.VMEM((asked, width), half_type),
                pltpu.VMEM((width, width), half_type),
                pltpu.VMEM((width, width), half_type),
                pltpu.VMEM((HEADS, count, HD), half_type),
                pltpu.VMEM((HEADS, count, HD), half_type),
                pltpu.VMEM((HEADS, asked, HD), half_type),
                whole,
                whole,
                whole,
                pltpu.VMEM((MATS, n_view - 1, FF, HD), half_type),
                whole,
                pltpu.VMEM((MATS, n_patch - 1, piece, HD), half_type),
                whole,
                whole,
                pltpu.VMEM((asked, width), fp),
                pltpu.SemaphoreType.DMA((4 + 3 * HEADS,)),
                pltpu.SemaphoreType.DMA((MATS, slots)),
                pltpu.SemaphoreType.DMA((MATS, slots)),
            ],
            compiler_params=pltpu.CompilerParams(
                collective_id=0, has_side_effects=True, vmem_limit_bytes=56 * 1024 * 1024
            ),
        )(
            tokens, w_kv, w_rate, jnp.transpose(fast_weights, (1, 2, 0, 3)),
            queries, w_query, out_gain, w_out,
        )

    shard = P(("groups", "patch", "view", "head"), None)
    in_specs = (shard, P(), P(), P(), shard, P(), P(), P())
    return jax.shard_map(local, mesh=mesh, in_specs=in_specs, out_specs=shard, check_vma=False)
```

```python
import functools

import jax
import jax.numpy as jnp
from jax import lax
from jax.experimental import pallas as pl
from jax.experimental.pallas import tpu as pltpu
from jax.sharding import PartitionSpec as P

HEADS = 3
HD = 256
FF = 512
STEPS = 3
KINDS = 3
MATS = KINDS * HEADS
D = HEADS * HD
MESH = pl.DeviceIdType.MESH

coef_a = 3.4445
coef_b = -4.775
coef_c = 2.0315
eta_rate = 3.0
eps_small = 1e-06
fp = jnp.float32
half_type = jnp.bfloat16


def dot_nn(a, b):
    return lax.dot_general(a, b, (((1,), (0,)), ((), ())), preferred_element_type=fp)


def dot_nt(a, b):
    return lax.dot_general(a, b, (((1,), (1,)), ((), ())), preferred_element_type=fp)


def dot_tn(a, b):
    return lax.dot_general(a, b, (((0,), (0,)), ((), ())), preferred_element_type=fp)


def unit(raw):
    return (raw * lax.rsqrt(jnp.sum(raw * raw, -1, keepdims=True) + eps_small)).astype(half_type)


def kernel(
    n_view, n_patch,
    tokens_hbm, w_kv_hbm, w_rate, fast_hbm, queries_hbm, w_query_hbm, gain, w_out_hbm, out,
    tokens, w_kv, fast, queries, w_query, w_out,
    keys, scaled, qry, grad, core_in, mid, view_in, low, patch_in, full, fresh, acc,
    load, send, recv,
):
    core, view, patch = lax.axis_index("head"), lax.axis_index("view"), lax.axis_index("patch")
    rounds, base = [], 0
    while 2 ** len(rounds) < n_patch:
        step = 2 ** len(rounds)
        size = FF // (2 * step)
        bit = lax.rem(patch // step, 2)
        kept, sent = base + bit * size, base + (1 - bit) * size
        rounds.append((patch + (1 - 2 * bit) * step, kept, sent, size))
        base = kept
    last_round = len(rounds) - 1
    loads = []

    def fetch(source, target):
        copy = pltpu.make_async_copy(source, target, load.at[len(loads)])
        copy.start()
        loads.append(copy)
        return copy

    get_tokens = fetch(tokens_hbm, tokens)
    get_kv, get_fast = [], []
    for h in range(HEADS):
        get_kv.append([
            fetch(w_kv_hbm.at[:, start:start + HD], w_kv.at[:, start:start + HD])
            for start in (h * HD, D + h * HD)
        ])
        get_fast.append(fetch(fast_hbm.at[:, h], fast.at[:, h]))
    get_query = [fetch(queries_hbm, queries), fetch(w_query_hbm, w_query)]
    get_out = fetch(w_out_hbm, w_out)

    barrier = pltpu.get_barrier_semaphore()
    pl.semaphore_signal(barrier, inc=1, device_id={"head": 1 - core}, device_id_type=MESH)
    for d in range(1, n_view):
        pl.semaphore_signal(
            barrier, inc=1, device_id={"view": lax.rem(view + d, n_view)}, device_id_type=MESH
        )
    for to, _, _, _ in rounds:
        pl.semaphore_signal(barrier, inc=1, device_id={"patch": to}, device_id_type=MESH)

    core_sum, core_share = 0, 1
    view_sum = 2
    view_share = view_sum + n_view - 1
    patch_sum = view_share + n_view - 1
    patch_share = patch_sum + n_patch - 1

    def owner(m):
        slot = m % (2 * n_view)
        return slot % n_view, slot // n_view

    def remote(m, slot, source, target, where):
        return pltpu.make_async_remote_copy(
            src_ref=source, dst_ref=target, send_sem=send.at[m, slot], recv_sem=recv.at[m, slot],
            device_id=where, device_id_type=MESH,
        )

    def sum_over_core(m):
        return remote(m, core_sum, grad.at[m], core_in.at[m], {"head": 1 - core})

    def sum_over_view(m, d):
        return remote(m, view_sum + d - 1, mid.at[m], view_in.at[m, d - 1], {"view": owner(m)[0]})

    def rows(start, size):
        return pl.ds(pl.multiple_of(start, 16), size)

    def arrived(m, r):
        size = rounds[r][3]
        return patch_in.at[m, FF - 2 * size:FF - size]

    def sum_over_patch(m, r):
        to, _, sent, size = rounds[r]
        return remote(m, patch_sum + r, low.at[m, rows(sent, size)], arrived(m, r), {"patch": to})

    def share_over_patch(m, r):
        to, kept, _, size = rounds[r]
        own = full.at[m, rows(kept, size)]
        return remote(m, patch_share + r, own, own, {"patch": to})

    def share_over_view(m, d):
        to = (owner(m)[0] + d) % n_view
        return remote(m, view_share + d - 1, fresh.at[m], fresh.at[m], {"view": to})

    def share_over_core(m):
        return remote(m, core_share, fresh.at[m], fresh.at[m], {"head": 1 - core})

    def at_owner(m):
        return jnp.logical_and(core == owner(m)[1], view == owner(m)[0])

    def at_view(m, v):
        return jnp.logical_and(core == owner(m)[1], view == v % n_view)

    def gradient(h):
        get_fast[h].wait()
        key, val = keys[h], scaled[h]
        gate_pre = dot_nt(fast[0, h], key)
        up_pre = dot_nt(fast[1, h], key)
        back = dot_nt(fast[2, h], val)
        sig = jax.nn.sigmoid(gate_pre)
        act = gate_pre * sig
        hidden = (act * up_pre).astype(half_type)
        d_gate = (back * up_pre * sig * (1.0 + gate_pre * (1.0 - sig))).astype(half_type)
        d_up = (back * act).astype(half_type)
        grad[h * KINDS] = dot_nn(d_gate, key).astype(half_type)
        grad[h * KINDS + 1] = dot_nn(d_up, key).astype(half_type)
        grad[h * KINDS + 2] = dot_nn(hidden, val).astype(half_type)

    def stage_core(m):
        @pl.when(core != owner(m)[1])
        def _():
            sum_over_core(m).start()

    def stage_view(m):
        @pl.when(core == owner(m)[1])
        def _():
            sum_over_core(m).wait_recv()
            mid[m] = (grad[m].astype(fp) + core_in[m].astype(fp)).astype(half_type)

        for d in range(1, n_view):
            @pl.when(at_view(m, owner(m)[0] - d))
            def _():
                sum_over_view(m, d).start()

    def stage_patch(m):
        @pl.when(at_owner(m))
        def _():
            total = mid[m].astype(fp)
            for d in range(1, n_view):
                sum_over_view(m, d).wait_recv()
                total = total + view_in[m, d - 1].astype(fp)
            low[m] = total.astype(half_type)
            sum_over_patch(m, 0).start()

    def stage_halve(m, r):
        @pl.when(at_owner(m))
        def _():
            _, kept, _, size = rounds[r]
            own = rows(kept, size)
            sum_over_patch(m, r).wait_recv()
            total = (low[m, own].astype(fp) + arrived(m, r)[...].astype(fp)).astype(half_type)
            if r < last_round:
                low[m, own] = total
                sum_over_patch(m, r + 1).start()
            else:
                full[m, own] = total
                share_over_patch(m, r).start()

    def stage_double(m, r):
        @pl.when(at_owner(m))
        def _():
            share_over_patch(m, r).wait_recv()
            share_over_patch(m, r - 1).start()

    def newton(x):
        gram = dot_tn(x, x).astype(half_type)
        poly = (coef_b * gram.astype(fp) + coef_c * dot_nn(gram, gram)).astype(half_type)
        return (coef_a * x.astype(fp) + dot_nn(x, poly)).astype(half_type)

    def stage_update(m):
        @pl.when(at_owner(m))
        def _():
            share_over_patch(m, 0).wait_recv()
            summed = full[m].astype(fp)
            norm = jnp.sqrt(jnp.sum(summed * summed, keepdims=True)) + eps_small
            ortho = (summed * (1.0 / norm)).astype(half_type)
            for _ in range(STEPS):
                ortho = newton(ortho)
            old = fast[m % KINDS, m // KINDS].astype(fp)
            moved = old + eta_rate * ortho.astype(fp)
            old_norm = jnp.sqrt(jnp.sum(old * old, -1, keepdims=True))
            new_norm = jnp.sqrt(jnp.sum(moved * moved, -1, keepdims=True)) + eps_small
            fresh[m] = (moved * (old_norm / new_norm)).astype(half_type)
            for d in range(1, n_view):
                share_over_view(m, d).start()
            share_over_core(m).start()

    def stage_spread(m):
        for d in range(1, n_view):
            @pl.when(at_view(m, owner(m)[0] + d))
            def _():
                share_over_view(m, d).wait_recv()
                share_over_core(m).start()

    def decode(h):
        for m in range(h * KINDS, (h + 1) * KINDS):
            @pl.when(core != owner(m)[1])
            def _():
                share_over_core(m).wait_recv()
        gate_pre = dot_nt(qry[h], fresh[h * KINDS])
        up_pre = dot_nt(qry[h], fresh[h * KINDS + 1])
        q_hidden = (gate_pre * jax.nn.sigmoid(gate_pre) * up_pre).astype(half_type)
        read = dot_nn(q_hidden, fresh[h * KINDS + 2])
        normed = read * lax.rsqrt(jnp.mean(read * read, -1, keepdims=True) + eps_small)
        normed = (normed * gain[h * HD:(h + 1) * HD].astype(fp)[None, :]).astype(half_type)
        term = dot_nn(normed, w_out[h * HD:(h + 1) * HD, :])
        if h == 0:
            acc[...] = term
        elif h < HEADS - 1:
            acc[...] += term
        else:
            out[...] = (acc[...] + term).astype(half_type)

    def finish(m):
        @pl.when(core != owner(m)[1])
        def _():
            sum_over_core(m).wait_send()

        for d in range(1, n_view):
            @pl.when(at_view(m, owner(m)[0] - d))
            def _():
                sum_over_view(m, d).wait_send()

        @pl.when(at_owner(m))
        def _():
            for r in range(len(rounds)):
                sum_over_patch(m, r).wait_send()
                share_over_patch(m, r).wait_send()
            for d in range(1, n_view):
                share_over_view(m, d).wait_send()

        @pl.when(core == owner(m)[1])
        def _():
            share_over_core(m).wait_send()

    get_tokens.wait()
    rate_pre = dot_nt(tokens[...], w_rate[...])
    rate = jnp.maximum(rate_pre, 0.0) + jnp.log1p(jnp.exp(-jnp.abs(rate_pre)))
    first, second, last = [range(h * KINDS, (h + 1) * KINDS) for h in range(HEADS)]

    def project(h):
        for copy in get_kv[h]:
            copy.wait()
        keys[h] = unit(dot_nn(tokens[...], w_kv[:, h * HD:(h + 1) * HD]))
        values = dot_nn(tokens[...], w_kv[:, D + h * HD:D + (h + 1) * HD])
        scaled[h] = (rate[:, h:h + 1] * values).astype(half_type)

    def run(stage, chosen):
        for m in chosen:
            stage(m)

    project(0)
    gradient(0)
    pl.semaphore_wait(barrier, n_view + len(rounds))
    run(stage_core, first)
    project(1)
    run(stage_view, first)
    gradient(1)
    run(stage_core, second)
    project(2)
    run(stage_view, second)
    gradient(2)
    run(stage_core, last)
    for copy in get_query:
        copy.wait()
    for h in range(HEADS):
        qry[h] = unit(dot_nn(queries[...], w_query[:, h * HD:(h + 1) * HD]))
        if h == 0:
            run(stage_view, last)
    get_out.wait()
    early, late, rest = range(0, 4), range(4, 8), range(8, MATS)
    def halve(chosen, r):
        for m in chosen:
            stage_halve(m, r)

    def double(chosen):
        for r in range(last_round, 0, -1):
            for m in chosen:
                stage_double(m, r)

    run(stage_patch, early)
    for r in range(last_round + 1):
        halve(early, r)
    run(stage_patch, late)
    double(early)
    halve(late, 0)
    run(stage_update, early)
    for r in range(1, last_round + 1):
        halve(late, r)
    run(stage_patch, rest)
    double(late)
    for r in range(last_round + 1):
        halve(rest, r)
    double(rest)
    run(stage_spread, early)
    run(stage_update, late)
    run(stage_update, rest)
    run(stage_spread, late)
    decode(0)
    decode(1)
    run(stage_spread, rest)
    decode(2)
    run(finish, range(MATS))


def solution(mesh):
    n_view, n_patch = mesh.shape["view"], mesh.shape["patch"]
    slots = 2 * (n_view + n_patch - 1)

    def local(tokens, w_kv, w_rate, fast_weights, queries, w_query, out_gain, w_out):
        count, width = tokens.shape
        asked = queries.shape[0]
        vmem = pl.BlockSpec(memory_space=pltpu.VMEM)
        hbm = pl.BlockSpec(memory_space=pl.ANY)
        whole = pltpu.VMEM((MATS, FF, HD), half_type)
        return pl.pallas_call(
            functools.partial(kernel, n_view, n_patch),
            out_shape=jax.ShapeDtypeStruct((asked, width), half_type),
            in_specs=[hbm, hbm, vmem, hbm, hbm, hbm, vmem, hbm],
            out_specs=vmem,
            scratch_shapes=[
                pltpu.VMEM((count, width), half_type),
                pltpu.VMEM((width, 2 * width), half_type),
                pltpu.VMEM((KINDS, HEADS, FF, HD), half_type),
                pltpu.VMEM((asked, width), half_type),
                pltpu.VMEM((width, width), half_type),
                pltpu.VMEM((width, width), half_type),
                pltpu.VMEM((HEADS, count, HD), half_type),
                pltpu.VMEM((HEADS, count, HD), half_type),
                pltpu.VMEM((HEADS, asked, HD), half_type),
                whole,
                whole,
                whole,
                pltpu.VMEM((MATS, n_view - 1, FF, HD), half_type),
                whole,
                whole,
                whole,
                whole,
                pltpu.VMEM((asked, width), fp),
                pltpu.SemaphoreType.DMA((4 + 3 * HEADS,)),
                pltpu.SemaphoreType.DMA((MATS, slots)),
                pltpu.SemaphoreType.DMA((MATS, slots)),
            ],
            compiler_params=pltpu.CompilerParams(
                collective_id=0, has_side_effects=True, vmem_limit_bytes=56 * 1024 * 1024
            ),
        )(
            tokens, w_kv, w_rate, jnp.transpose(fast_weights, (1, 2, 0, 3)),
            queries, w_query, out_gain, w_out,
        )

    shard = P(("groups", "patch", "view", "head"), None)
    in_specs = (shard, P(), P(), P(), shard, P(), P(), P())
    return jax.shard_map(local, mesh=mesh, in_specs=in_specs, out_specs=shard, check_vma=False)
```
